512 devices in a mesh: ctx: 64 (over z, y_hi, x), ch: 8 (over y_lo, core).
Axes of the slice: x: 4, y: 8 (y_hi: 2, y_lo: 4; y = y_hi * 4 + y_lo), z: 8, core: 2. Of those that a mesh axis runs over, the one named last changes fastest.
Arguments:
- post_gate: bfloat16 [2, 4096, 8192], P(None, 'ctx', 'ch'), may hold values from -6 to 6
- pre_gate: bfloat16 [2, 4096, 8192], P(None, 'ctx', 'ch'), may hold values from -6 to 6
- signal: bfloat16 [2, 4096, 8192], P(None, 'ctx', 'ch'), may hold values from -6 to 6
- long_filter: bfloat16 [4096, 8192], P('ctx', 'ch'), may hold values from -1 to 1
- out_weight: bfloat16 [8192, 4096], P('ch', 'ctx'), may hold values from -0.0625 to 0.0625
Outputs:
- layer_out: bfloat16 [2, 4096, 4096], P(None, 'ctx', 'ch')
The draws below stay inside these ranges and needn't reach their ends.
All inputs are finite; a program needn't handle non-finite values.
Results may differ from the reference program's by a relative error of at most 0.025.
Values may be sent and summed in bfloat16 or wider, within the bound.
A program may use at most 64 MiB of HBM per device.

```python
import math
import jax
import jax.numpy as jnp
from jax import lax

D = 8192
OUT_COLS = 4096
SEQS = 2
TOK_DEV = 64
LENGTH = 4096
N_CTX = 64
N_CH = 8


def draw_long_filter(key, part):
    key = jax.random.fold_in(key, 7)
    rate_key, noise_key = jax.random.split(key)
    low, high = (math.log(0.3 / LENGTH), math.log(1.0 / 30.0))
    rate = jnp.exp(jax.random.uniform(rate_key, (D,), jnp.float32, low, high))
    steps = jnp.arange(LENGTH, dtype=jnp.float32)
    envelope = jnp.exp(-steps[:, None] * rate[None, :])
    amplitude = jnp.sqrt(1.0 - jnp.exp(-2.0 * rate))
    noise = jnp.clip(jax.random.normal(noise_key, (LENGTH, D), jnp.float32), -3.9, 3.9)
    return (amplitude[None, :] * envelope * noise).astype(jnp.bfloat16)


def steps_of(stream_key, extent, cuts, low, largest):
    def one(axis_at, blocks):
        draws = jax.random.uniform(jax.random.fold_in(jax.random.fold_in(stream_key, 6), axis_at), (blocks,), jnp.float32, low / len(cuts), largest / len(cuts))
        return jnp.repeat(jnp.exp(draws), extent[axis_at] // blocks).reshape((-1,) + (1,) * (len(extent) - axis_at - 1))

    factor_of = one(*cuts[0])
    for cut in cuts[1:]:
        factor_of = factor_of * one(*cut)
    return factor_of


def gaussian(rng, extent, deviation, limit, cuts=(), kind=jnp.bfloat16):
    entries = jax.random.normal(rng, extent, jnp.float32) * deviation
    if len(cuts) > 0:
        entries = steps_of(rng, extent, cuts, -0.22, 0.18) * entries
    return jnp.clip(entries, min=-limit, max=limit).astype(kind)


def setup_inputs(seed: int = 0) -> dict:
    arg_keys = jax.random.split(jax.random.key(seed), 6)
    post_gate = gaussian(arg_keys[0], (SEQS, LENGTH, D), 1.0, 6.0, ((1, 64), (2, 8)))
    pre_gate = gaussian(arg_keys[1], (SEQS, LENGTH, D), 1.0, 6.0, ((1, 64), (2, 8)))
    signal = gaussian(arg_keys[2], (SEQS, LENGTH, D), 1.0, 6.0, ((1, 64), (2, 8)))
    long_filter = draw_long_filter(jax.random.fold_in(arg_keys[5], 71), 0)
    out_weight = gaussian(arg_keys[4], (D, OUT_COLS), D ** -0.5, 0.0625, ((0, 8), (1, 64)))
    return dict(post_gate=post_gate, pre_gate=pre_gate, signal=signal, long_filter=long_filter, out_weight=out_weight)


def settle(values):
    return lax.optimization_barrier(values.astype(jnp.bfloat16)).astype(jnp.float32)


def twiddle(count, width, span):
    freq = jnp.arange(count, dtype=jnp.int32)
    inner = jnp.arange(width, dtype=jnp.int32)
    product = (freq[:, None] * inner[None, :]) % span
    theta = product.astype(jnp.float32) * (2.0 * math.pi / span)
    return jnp.cos(theta)[None, :, :, None], jnp.sin(theta)[None, :, :, None]


def conv_block(inner_block, filter_block):
    blocks = N_CTX
    width = TOK_DEV
    span = 2 * blocks * width
    stacked = jnp.concatenate([filter_block[None], inner_block], axis=0).astype(jnp.float32)
    stacked = stacked.reshape(stacked.shape[0], blocks, width, stacked.shape[-1])
    first = jnp.fft.fft(stacked, n=2 * blocks, axis=1)
    cos_tw, sin_tw = twiddle(2 * blocks, width, span)
    first_real = settle(jnp.real(first) * cos_tw + jnp.imag(first) * sin_tw)
    first_imag = settle(jnp.imag(first) * cos_tw - jnp.real(first) * sin_tw)
    spectrum = jnp.fft.fft(first_real + 1j * first_imag, axis=2)
    product = spectrum[0:1] * spectrum[1:]
    middle = jnp.fft.ifft(product, axis=2) * width
    back_real = settle(jnp.real(middle) * cos_tw - jnp.imag(middle) * sin_tw)
    back_imag = settle(jnp.imag(middle) * cos_tw + jnp.real(middle) * sin_tw)
    summed = jnp.fft.ifft(back_real + 1j * back_imag, axis=1) * (2 * blocks)
    convolved = (jnp.real(summed)[:, :blocks] / span).astype(jnp.bfloat16)
    return convolved.reshape(convolved.shape[0], blocks * width, convolved.shape[-1])


def reference(post_gate, pre_gate, signal, long_filter, out_weight):
    group_width = D // N_CH
    inner = (pre_gate.astype(jnp.float32) * signal.astype(jnp.float32)).astype(jnp.bfloat16)
    seqs, length = inner.shape[0], inner.shape[1]
    inner_groups = jnp.transpose(inner.reshape(seqs, length, N_CH, group_width), (2, 0, 1, 3))
    filter_groups = jnp.transpose(long_filter.reshape(length, N_CH, group_width), (1, 0, 2))
    convolved = lax.map(lambda pair: conv_block(pair[0], pair[1]), (inner_groups, filter_groups))
    convolved = jnp.transpose(convolved, (1, 2, 0, 3)).reshape(seqs, length, D)
    gated = (post_gate.astype(jnp.float32) * convolved.astype(jnp.float32)).astype(jnp.bfloat16)
    flat = gated.reshape(seqs * length, D)
    total = jnp.zeros((seqs * length, OUT_COLS), jnp.float32)
    for group in range(N_CH):
        lo = group * group_width
        partial_value = jnp.dot(flat[:, lo:lo + group_width], out_weight[lo:lo + group_width], preferred_element_type=jnp.float32)
        total = total + settle(partial_value)
    return total.astype(jnp.bfloat16).reshape(seqs, length, OUT_COLS)
```

```python
import functools
import math

import jax
import jax.numpy as jnp
import numpy as np
from jax import lax
from jax.experimental import pallas as pl
from jax.experimental.pallas import tpu as pltpu
from jax.sharding import PartitionSpec as P

MESH = pl.DeviceIdType.MESH
F32 = jnp.float32
BF16 = jnp.bfloat16


def tables():
    n1, n2, span = 128, 64, 8192
    k1 = np.arange(n1)
    b = np.arange(64)
    j = np.arange(n2)
    th = 2 * math.pi * ((k1[:, None] * b[None, :]) % n1) / n1
    cs = np.concatenate([np.cos(th), np.sin(th)], 1)
    ph = 2 * math.pi * ((k1[:, None] * j[None, :]) % span) / span
    c, s = np.cos(ph), np.sin(ph)
    tc = np.concatenate([c, c], 1)
    ts = np.concatenate([s, -s], 1)
    tcn = np.concatenate([-c, c], 1)
    tsn = np.concatenate([-s, -s], 1)
    twid = np.stack([tc, ts, tcn, tsn])
    t2 = 2 * math.pi * ((j[:, None] * j[None, :]) % n2) / n2
    c2, s2 = np.cos(t2), np.sin(t2)
    fwd = np.block([[c2, -s2, -s2, c2], [s2, c2, c2, s2]])
    filt = np.block([[c2, c2, s2, -s2], [s2, s2, -c2, c2]])
    inv = np.block([[c2, s2, s2, c2], [-s2, c2, c2, -s2]])
    mid = np.stack([fwd, filt, inv])
    last = np.concatenate([np.cos(th.T), np.sin(th.T)], 1) / span
    return (
        jnp.asarray(cs, BF16),
        jnp.asarray(twid, F32),
        jnp.asarray(mid, BF16),
        jnp.asarray(last, BF16),
    )


def kernel(
    pre_h, sig_h, fil_h, post_h, w_h, cs_h, tw_h, mid_h, last_h,
    out,
    pre, sig, fil, post, w, cs, tw, mid, last,
    msg1, rcv1, xf, of, msg2, rcv2, post_t, post_r, lhs, wall, half, rcv3, own, summ, rcv4,
    in_sem, s1, r1, wy_s, wy_r, wz_s, wz_r, ps, pr, s2, r2, gs, gr, es, er, fs, fr,
):
    me = lax.axis_index("ctx")
    ch = lax.axis_index("ch")
    x = lax.rem(me, 4)
    zy = me // 4
    h = lax.rem(zy, 2)
    z = zy // 2
    core = lax.rem(ch, 2)
    yl = ch // 2

    loads = []
    for i, (src, dst) in enumerate(
        [(pre_h, pre), (sig_h, sig), (fil_h, fil), (w_h, w), (post_h, post),
         (cs_h, cs), (tw_h, tw), (mid_h, mid), (last_h, last)]
    ):
        cp = pltpu.make_async_copy(src, dst, in_sem.at[i])
        cp.start()
        loads.append(cp)

    barrier = pltpu.get_barrier_semaphore()

    def greet(k, carry):
        pl.semaphore_signal(barrier, inc=1, device_id=(lax.rem(me + k, 64), ch), device_id_type=MESH)
        return carry

    lax.fori_loop(1, 64, greet, 0)

    def greet2(k, carry):
        px = lax.rem(x + lax.rem(k, 4), 4)
        py = lax.rem(yl + k // 4, 4)
        pl.semaphore_signal(
            barrier, inc=1, device_id=(zy * 4 + px, py * 2 + core), device_id_type=MESH
        )
        return carry

    lax.fori_loop(4, 16, greet2, 0)
    pl.semaphore_signal(barrier, inc=1, device_id=(me, yl * 2 + 1 - core), device_id_type=MESH)

    low = lax.broadcasted_iota(jnp.int32, (8, 128), 1) < 64

    for i in range(3):
        loads[i].wait()
    for blk in range(8):
        lanes = slice(128 * blk, 128 * blk + 128)
        v = [
            (pre[s, :, lanes].astype(F32) * sig[s, :, lanes].astype(F32)).astype(BF16).astype(F32)
            for s in range(2)
        ]
        xt = jnp.concatenate(v, 0).T
        f = fil[:, lanes].astype(F32)
        ft = jnp.concatenate([f, f], 0).T
        for i in range(8):
            q = 8 * blk + i
            msg1[q, 0:16, :] = xt[16 * i : 16 * i + 16].astype(BF16)
            msg1[q, 16:24, :] = jnp.where(
                low, ft[16 * i : 16 * i + 8], ft[16 * i + 8 : 16 * i + 16]
            ).astype(BF16)

    pl.semaphore_wait(barrier, 76)

    def send1(k, carry):
        to = lax.rem(me + k, 64)
        q = lax.rem(to, 4) * 16 + to // 4
        pltpu.make_async_remote_copy(
            src_ref=msg1.at[q], dst_ref=rcv1.at[me], send_sem=s1, recv_sem=r1,
            device_id=(to, ch), device_id_type=MESH,
        ).start()
        return carry

    lax.fori_loop(1, 64, send1, 0)
    rcv1[me] = msg1[x * 16 + zy]

    loads[3].wait()
    for blk in range(8):
        wb = w[128 * blk : 128 * blk + 128, :].astype(F32)
        wall[zy, :, 128 * blk : 128 * blk + 128] = wb.T.astype(BF16)
    wy = pltpu.make_async_remote_copy(
        src_ref=wall.at[zy], dst_ref=wall.at[zy], send_sem=wy_s, recv_sem=wy_r,
        device_id=((zy + 1 - 2 * h) * 4 + x, ch), device_id_type=MESH,
    )
    wy.start()

    loads[4].wait()
    for blk in range(8):
        lanes = slice(128 * blk, 128 * blk + 128)
        pt = jnp.concatenate([post[s, :, lanes].astype(F32) for s in range(2)], 0).T
        for i in range(8):
            post_t[8 * blk + i] = pt[16 * i : 16 * i + 16].astype(BF16)

    def post_copy(d):
        px = lax.rem(x + d, 4)
        return pltpu.make_async_remote_copy(
            src_ref=post_t.at[pl.ds(16 * px, 16)], dst_ref=post_r.at[x], send_sem=ps, recv_sem=pr,
            device_id=(zy * 4 + px, ch), device_id_type=MESH,
        )

    for d in range(1, 4):
        post_copy(d).start()
    post_r[x] = post_t[pl.ds(16 * x, 16)]

    def ring(step):
        right_z, left_z = lax.rem(z + 1, 8), lax.rem(z + 7, 8)
        pair_r = lax.rem(z + 8 - step + 1, 8)
        pair_l = lax.rem(z + step - 1, 8)
        if step < 4:
            part_r, part_l = pl.ds(2 * pair_r, 2), pl.ds(2 * pair_l, 2)
        else:
            part_r, part_l = pl.ds(2 * pair_r, 1), pl.ds(2 * pair_l + 1, 1)
        to_right = pltpu.make_async_remote_copy(
            src_ref=wall.at[part_r], dst_ref=wall.at[part_r],
            send_sem=wz_s.at[2 * step - 2], recv_sem=wz_r.at[2 * step - 2],
            device_id=((right_z * 2 + h) * 4 + x, ch), device_id_type=MESH,
        )
        to_left = pltpu.make_async_remote_copy(
            src_ref=wall.at[part_l], dst_ref=wall.at[part_l],
            send_sem=wz_s.at[2 * step - 1], recv_sem=wz_r.at[2 * step - 1],
            device_id=((left_z * 2 + h) * 4 + x, ch), device_id_type=MESH,
        )
        return to_right, to_left

    rings = [ring(i) for i in range(1, 5)]
    wy.wait_recv()
    for cp in rings[0]:
        cp.start()

    for i in range(5, 9):
        loads[i].wait()
    pltpu.make_async_remote_copy(
        src_ref=msg1.at[pl.ds(0, 63)], dst_ref=rcv1.at[pl.ds(0, 63)], send_sem=s1, recv_sem=r1,
        device_id=(me, ch), device_id_type=MESH,
    ).wait_recv()

    def widen(b, carry):
        xf[pl.ds(pl.multiple_of(b * 24, 8), 24), :] = rcv1[b].astype(F32)
        return carry

    lax.fori_loop(0, 64, widen, 0, unroll=8)

    for cp in rings[0]:
        cp.wait_recv()
    for cp in rings[1]:
        cp.start()

    wide_low = lax.broadcasted_iota(jnp.int32, (64, 128), 1) < 64
    sign = jnp.where(wide_low, 1.0, -1.0).astype(F32)
    zero = jnp.zeros((64, 128), F32)

    def pair(c, carry):
        g = xf[pl.ds(16 + c, 64, stride=24), :]
        rg = pltpu.roll(g, 64, 1)
        for part in range(2):
            v = xf[pl.ds(c + 8 * part, 64, stride=24), :]
            r = pltpu.roll(v, 64, 1)
            own_h, oth_h = (g, rg) if part == 0 else (rg, g)
            lo = jnp.where(wide_low, own_h, zero)
            hi = jnp.where(wide_low, zero, oth_h)
            top = jnp.concatenate([v, r, lo, hi], 1).astype(BF16)
            bot = jnp.concatenate([r * sign, -v * sign, -hi, -lo], 1).astype(BF16)
            a = jnp.dot(cs[...], jnp.concatenate([top, bot], 0), preferred_element_type=F32)
            tc, ts = tw[0], tw[1]
            sg = (a[:, 0:128] * tc + a[:, 128:256] * ts).astype(BF16)
            fg = (a[:, 256:384] * tc + a[:, 384:512] * ts).astype(BF16)
            zz = jnp.dot(sg, mid[0], preferred_element_type=F32)
            hh = jnp.dot(fg, mid[1], preferred_element_type=F32)
            p = (zz[:, 0:128] * hh[:, 0:128] + zz[:, 128:256] * hh[:, 128:256]).astype(BF16)
            m = jnp.dot(p, mid[2], preferred_element_type=F32)
            m0, m1 = m[:, 0:128], m[:, 128:256]
            back = jnp.concatenate(
                [(m0 * tc - m1 * ts).astype(BF16), (m1 * tw[2] + m0 * tw[3]).astype(BF16)], 0
            )
            of[pl.ds(c + 8 * part, 64, stride=16), :] = jnp.dot(
                last[...], back, preferred_element_type=F32
            )
        return carry

    lax.fori_loop(0, 4, pair, 0)
    for cp in rings[1]:
        cp.wait_recv()
    for cp in rings[2]:
        cp.start()
    lax.fori_loop(4, 8, pair, 0)

    def narrow(b, carry):
        msg2[b] = of[pl.ds(pl.multiple_of(b * 16, 16), 16), :].astype(BF16)
        return carry

    lax.fori_loop(0, 64, narrow, 0, unroll=8)

    def send2(k, carry):
        to = lax.rem(zy + k, 16)
        pltpu.make_async_remote_copy(
            src_ref=msg2.at[pl.ds(4 * to, 4)], dst_ref=rcv2.at[zy], send_sem=s2, recv_sem=r2,
            device_id=(to * 4 + x, ch), device_id_type=MESH,
        ).start()
        return carry

    lax.fori_loop(1, 16, send2, 0)
    rcv2[zy] = msg2[pl.ds(4 * zy, 4)]

    pltpu.make_async_remote_copy(
        src_ref=post_r.at[pl.ds(0, 3)], dst_ref=post_r.at[pl.ds(0, 3)], send_sem=ps, recv_sem=pr,
        device_id=(me, ch), device_id_type=MESH,
    ).wait_recv()
    for cp in rings[2]:
        cp.wait_recv()
    for cp in rings[3]:
        cp.start()
    pltpu.make_async_remote_copy(
        src_ref=rcv2.at[pl.ds(0, 15)], dst_ref=rcv2.at[pl.ds(0, 15)], send_sem=s2, recv_sem=r2,
        device_id=(me, ch), device_id_type=MESH,
    ).wait_recv()

    for px in range(4):
        gt = (rcv2[:, px].astype(F32) * post_r[px].astype(F32)).astype(BF16).astype(F32)
        gt = gt.reshape(256, 128)
        for i in range(2):
            lhs[
                128 * px : 128 * px + 128,
                pl.ds(pl.multiple_of(256 * x + 128 * i, 128), 128),
            ] = gt[128 * i : 128 * i + 128].T.astype(BF16)

    def gather(d):
        px = lax.rem(x + d, 4)
        mine = lhs.at[:, pl.ds(pl.multiple_of(256 * x, 256), 256)]
        return pltpu.make_async_remote_copy(
            src_ref=mine, dst_ref=mine, send_sem=gs.at[d - 1], recv_sem=gr.at[d - 1],
            device_id=(zy * 4 + px, ch), device_id_type=MESH,
        )

    gathers = [gather(d) for d in range(1, 4)]
    for cp in gathers:
        cp.start()
    for cp in rings[3]:
        cp.wait_recv()
    for cp in gathers:
        cp.wait_recv()

    sib = (me, yl * 2 + 1 - core)

    def swap(y):
        return pltpu.make_async_remote_copy(
            src_ref=half.at[y], dst_ref=rcv3.at[y], send_sem=es.at[y], recv_sem=er.at[y],
            device_id=sib, device_id_type=MESH,
        )

    def columns(y, c):
        return wall[pl.ds(4 * y + 2 * c, 2)].reshape(128, 1024)

    dims = (((1,), (1,)), ((), ()))
    for yp in range(2):
        wt = jnp.concatenate([columns(2 * yp, 1 - core), columns(2 * yp + 1, 1 - core)], 0)
        acc = lax.dot_general(lhs[...], wt, dims, preferred_element_type=F32)
        half[2 * yp] = acc[:, 0:128].astype(BF16)
        half[2 * yp + 1] = acc[:, 128:256].astype(BF16)
        swap(2 * yp).start()
        swap(2 * yp + 1).start()
    for yp in range(2):
        wt = jnp.concatenate([columns(2 * yp, core), columns(2 * yp + 1, core)], 0)
        acc = lax.dot_general(lhs[...], wt, dims, preferred_element_type=F32)
        own[2 * yp] = acc[:, 0:128]
        own[2 * yp + 1] = acc[:, 128:256]

    for y in range(4):
        swap(y).wait_recv()
        summ[y] = (own[y] + rcv3[y].astype(F32)).astype(BF16)

    def last_send(k, carry):
        px = lax.rem(x + lax.rem(k, 4), 4)
        py = lax.rem(yl + k // 4, 4)
        pltpu.make_async_remote_copy(
            src_ref=summ.at[py, pl.ds(pl.multiple_of(128 * px, 128), 128)],
            dst_ref=rcv4.at[x * 4 + yl], send_sem=fs, recv_sem=fr,
            device_id=(zy * 4 + px, py * 2 + core), device_id_type=MESH,
        ).start()
        return carry

    lax.fori_loop(1, 16, last_send, 0)
    rcv4[x * 4 + yl] = summ[yl, pl.ds(pl.multiple_of(128 * x, 128), 128)]
    pltpu.make_async_remote_copy(
        src_ref=rcv4.at[pl.ds(0, 15)], dst_ref=rcv4.at[pl.ds(0, 15)], send_sem=fs, recv_sem=fr,
        device_id=(me, ch), device_id_type=MESH,
    ).wait_recv()

    t = []
    for px in range(4):
        v = rcv4[4 * px].astype(F32)
        for y in range(1, 4):
            v = v + rcv4[4 * px + y].astype(F32)
        t.append(v)
    row_low = lax.broadcasted_iota(jnp.int32, (128, 128), 1) < 64
    for m in range(4):
        a, b = t[(2 * m) % 4], t[(2 * m + 1) % 4]
        if m < 2:
            o = jnp.where(row_low, a, pltpu.roll(b, 64, 1))
        else:
            o = jnp.where(row_low, pltpu.roll(a, 64, 1), b)
        o = o.astype(BF16)
        out[0, :, 128 * m : 128 * m + 128] = o[0:64]
        out[1, :, 128 * m : 128 * m + 128] = o[64:128]

    pltpu.make_async_remote_copy(
        src_ref=msg1.at[pl.ds(0, 63)], dst_ref=rcv1.at[pl.ds(0, 63)], send_sem=s1, recv_sem=r1,
        device_id=(me, ch), device_id_type=MESH,
    ).wait_send()
    wy.wait_send()
    for pr_ in rings:
        for cp in pr_:
            cp.wait_send()
    pltpu.make_async_remote_copy(
        src_ref=post_r.at[pl.ds(0, 3)], dst_ref=post_r.at[pl.ds(0, 3)], send_sem=ps, recv_sem=pr,
        device_id=(me, ch), device_id_type=MESH,
    ).wait_send()
    pltpu.make_async_remote_copy(
        src_ref=rcv2.at[pl.ds(0, 15)], dst_ref=rcv2.at[pl.ds(0, 15)], send_sem=s2, recv_sem=r2,
        device_id=(me, ch), device_id_type=MESH,
    ).wait_send()
    for cp in gathers:
        cp.wait_send()
    for y in range(4):
        swap(y).wait_send()
    pltpu.make_async_remote_copy(
        src_ref=rcv4.at[pl.ds(0, 15)], dst_ref=rcv4.at[pl.ds(0, 15)], send_sem=fs, recv_sem=fr,
        device_id=(me, ch), device_id_type=MESH,
    ).wait_send()


def on_device(post_gate, pre_gate, signal, long_filter, out_weight):
    cs, tw, mid, last = tables()
    vm = pltpu.VMEM
    dma = pltpu.SemaphoreType.DMA
    scratch = [
        vm((2, 64, 1024), BF16), vm((2, 64, 1024), BF16), vm((64, 1024), BF16),
        vm((2, 64, 1024), BF16), vm((1024, 64), BF16),
        vm((128, 128), BF16), vm((4, 128, 128), F32), vm((3, 128, 256), BF16), vm((64, 256), BF16),
        vm((64, 24, 128), BF16),
        vm((64, 24, 128), BF16),
        vm((1536, 128), F32),
        vm((1024, 128), F32),
        vm((64, 16, 128), BF16),
        vm((16, 4, 16, 128), BF16),
        vm((64, 16, 128), BF16),
        vm((4, 16, 16, 128), BF16),
        vm((512, 1024), BF16),
        vm((16, 64, 1024), BF16),
        vm((4, 512, 128), BF16),
        vm((4, 512, 128), BF16),
        vm((4, 512, 128), F32),
        vm((4, 512, 128), BF16),
        vm((16, 128, 128), BF16),
        dma((9,)), dma, dma, dma, dma, dma((8,)), dma((8,)), dma, dma, dma, dma,
        dma((3,)), dma((3,)), dma((4,)), dma((4,)), dma, dma,
    ]
    return pl.pallas_call(
        kernel,
        out_shape=jax.ShapeDtypeStruct((2, 64, 512), BF16),
        in_specs=[pl.BlockSpec(memory_space=pl.ANY)] * 9,
        out_specs=pl.BlockSpec(memory_space=pltpu.VMEM),
        scratch_shapes=scratch,
        compiler_params=pltpu.CompilerParams(
            collective_id=0, has_side_effects=True, vmem_limit_bytes=40 * 1024 * 1024
        ),
        cost_estimate=pl.CostEstimate(flops=2_000_000_000, bytes_accessed=4_000_000, transcendentals=0),
    )(pre_gate, signal, long_filter, post_gate, out_weight, cs, tw, mid, last)


def solution(mesh):
    return jax.shard_map(
        on_device,
        mesh=mesh,
        in_specs=(
            P(None, "ctx", "ch"),
            P(None, "ctx", "ch"),
            P(None, "ctx", "ch"),
            P("ctx", "ch"),
            P("ch", "ctx"),
        ),
        out_specs=P(None, "ctx", "ch"),
        check_vma=False,
    )
```

```python
import functools
import math

import jax
import jax.numpy as jnp
import numpy as np
from jax import lax
from jax.experimental import pallas as pl
from jax.experimental.pallas import tpu as pltpu
from jax.sharding import PartitionSpec as P

WT, POST = True, True
PLAN = {"scatter1": ("a1",), "filter0": ("a2",), "back0": ("b1",), "recv1": ("a3",), "back1": ("b2", "a4"), "gather0": ("b3",), "gather1": ("b4", "a5"), "matmul": ("b5",)}
WY_FIRST = False
MESH = pl.DeviceIdType.MESH
F32 = jnp.float32
BF16 = jnp.bfloat16


def tables():
    n1, n2, span = 128, 64, 8192
    k1 = np.arange(n1)
    b = np.arange(64)
    j = np.arange(n2)
    th = 2 * math.pi * ((k1[:, None] * b[None, :]) % n1) / n1
    cs = np.concatenate([np.cos(th), np.sin(th)], 1)
    ph = 2 * math.pi * ((k1[:, None] * j[None, :]) % span) / span
    c, s = np.cos(ph), np.sin(ph)
    tc = np.concatenate([c, c], 1)
    ts = np.concatenate([s, -s], 1)
    tcn = np.concatenate([-c, c], 1)
    tsn = np.concatenate([-s, -s], 1)
    twid = np.stack([tc, ts, tcn, tsn])
    t2 = 2 * math.pi * ((j[:, None] * j[None, :]) % n2) / n2
    c2, s2 = np.cos(t2), np.sin(t2)
    fwd = np.block([[c2, -s2, -s2, c2], [s2, c2, c2, s2]])
    filt = np.block([[c2, c2, s2, -s2], [s2, s2, -c2, c2]])
    inv = np.block([[c2, s2, s2, c2], [-s2, c2, c2, -s2]])
    mid = np.stack([fwd, filt, inv])
    last = np.concatenate([np.cos(th.T), np.sin(th.T)], 1) / span
    return (
        jnp.asarray(cs, BF16),
        jnp.asarray(twid, F32),
        jnp.asarray(mid, BF16),
        jnp.asarray(last, BF16),
    )


def kernel(
    pre_h, sig_h, fil_h, post_h, w_h, cs_h, tw_h, mid_h, last_h,
    out,
    pre, sig, fil, post, cs, tw, mid, last,
    msg_a, rcv_a, msg_b, rcv_b, xa, xb, hf, st1, st2, st3, of, msg2, rcv2, post_t, post_r,
    lhs, wall, half, rcv3, own, summ, rcv4,
    in_sem, s1, r1, wy_s, wy_r, wa_s, wa_r, wb_s, wb_r, ps, pr, s2, r2, gs, gr, es, er, fs, fr,
):
    me = lax.axis_index("ctx")
    ch = lax.axis_index("ch")
    x = lax.rem(me, 4)
    zy = me // 4
    h = lax.rem(zy, 2)
    z = zy // 2
    core = lax.rem(ch, 2)
    yl = ch // 2
    slot = x * 16 + zy

    loads = []
    for i, (src, dst) in enumerate(
        [(pre_h, pre), (sig_h, sig), (fil_h, fil), (w_h, wall.at[zy]), (post_h, post),
         (cs_h, cs), (tw_h, tw), (mid_h, mid), (last_h, last)]
    ):
        cp = pltpu.make_async_copy(src, dst, in_sem.at[i])
        cp.start()
        loads.append(cp)

    barrier = pltpu.get_barrier_semaphore()

    def greet(k, carry):
        pl.semaphore_signal(barrier, inc=1, device_id=(lax.rem(me + k, 64), ch), device_id_type=MESH)
        return carry

    lax.fori_loop(1, 64, greet, 0)

    def greet2(k, carry):
        px = lax.rem(x + lax.rem(k, 4), 4)
        py = lax.rem(yl + k // 4, 4)
        pl.semaphore_signal(
            barrier, inc=1, device_id=(zy * 4 + px, py * 2 + core), device_id_type=MESH
        )
        return carry

    lax.fori_loop(4, 16, greet2, 0)
    pl.semaphore_signal(barrier, inc=1, device_id=(me, yl * 2 + 1 - core), device_id_type=MESH)

    low = lax.broadcasted_iota(jnp.int32, (8, 128), 1) < 64

    for i in range(3):
        loads[i].wait()
    for px in range(4):
        fts = []
        for c in range(2):
            lanes = slice(256 * px + 128 * c, 256 * px + 128 * c + 128)
            v = [
                (pre[s, :, lanes].astype(F32) * sig[s, :, lanes].astype(F32)).astype(BF16).astype(F32)
                for s in range(2)
            ]
            xt = jnp.concatenate(v, 0).T
            dst = (msg_a, msg_b)[c]
            for i in range(16):
                dst[16 * px + i, 0:8, :] = xt[8 * i : 8 * i + 8].astype(BF16)
            f = fil[:, lanes].astype(F32)
            fts.append(jnp.concatenate([f, f], 0).T)
        for i in range(16):
            msg_a[16 * px + i, 8:16, :] = jnp.where(
                low, fts[0][8 * i : 8 * i + 8], fts[1][8 * i : 8 * i + 8]
            ).astype(BF16)

    pl.semaphore_wait(barrier, 76)

    msgs, rcvs = (msg_a, msg_b), (rcv_a, rcv_b)

    def all1(c):
        return pltpu.make_async_remote_copy(
            src_ref=msgs[c].at[pl.ds(0, 63)], dst_ref=rcvs[c].at[pl.ds(0, 63)],
            send_sem=s1.at[c], recv_sem=r1.at[c], device_id=(me, ch), device_id_type=MESH,
        )

    def scatter(c):
        def send1(k, carry):
            to = lax.rem(me + k, 64)
            pltpu.make_async_remote_copy(
                src_ref=msgs[c].at[lax.rem(to, 4) * 16 + to // 4], dst_ref=rcvs[c].at[me],
                send_sem=s1.at[c], recv_sem=r1.at[c], device_id=(to, ch), device_id_type=MESH,
            ).start()
            return carry

        lax.fori_loop(1, 64, send1, 0)
        rcvs[c][me] = msgs[c][slot]

    wy = pltpu.make_async_remote_copy(
        src_ref=wall.at[zy], dst_ref=wall.at[zy], send_sem=wy_s, recv_sem=wy_r,
        device_id=((zy + 1 - 2 * h) * 4 + x, ch), device_id_type=MESH,
    )

    def ring(step, hh, ssem, rsem):
        right_z, left_z = lax.rem(z + 1, 8), lax.rem(z + 7, 8)
        from_r = 2 * lax.rem(z + 9 - step, 8) + hh
        from_l = 2 * lax.rem(z + step - 1, 8) + hh
        if step < 4:
            part_r, part_l = wall.at[from_r], wall.at[from_l]
        else:
            part_r, part_l = wall.at[from_r, pl.ds(0, 32)], wall.at[from_l, pl.ds(32, 32)]
        return [
            pltpu.make_async_remote_copy(
                src_ref=part, dst_ref=part,
                send_sem=ssem.at[2 * step - 2 + i], recv_sem=rsem.at[2 * step - 2 + i],
                device_id=((to * 2 + h) * 4 + x, ch), device_id_type=MESH,
            )
            for i, (part, to) in enumerate([(part_r, right_z), (part_l, left_z)])
        ]

    ring_a = [ring(i, h, wa_s, wa_r) for i in range(1, 5)]
    ring_b = [ring(i, 1 - h, wb_s, wb_r) for i in range(1, 5)]

    def step_w(which, i):
        if not WT:
            return
        rings = ring_a if which == "a" else ring_b
        if i > 1:
            for cp in rings[i - 2]:
                cp.wait_recv()
        elif which == "b":
            wy.wait_recv()
        if i < 5:
            for cp in rings[i - 1]:
                cp.start()

    def at(name):
        for op in PLAN.get(name, ()):
            step_w(op[0], int(op[1]))

    loads[3].wait()
    if WT and WY_FIRST:
        wy.start()
    scatter(0)
    at("scatter0")
    scatter(1)
    if WT and not WY_FIRST:
        wy.start()
    at("scatter1")

    loads[4].wait()
    for px in range(4):
        for c in range(2):
            lanes = slice(256 * px + 128 * c, 256 * px + 128 * c + 128)
            pt = jnp.concatenate([post[s, :, lanes].astype(F32) for s in range(2)], 0).T
            post_t[px, c] = pt.astype(BF16)

    def post_copy(d):
        px = lax.rem(x + d, 4)
        return pltpu.make_async_remote_copy(
            src_ref=post_t.at[px], dst_ref=post_r.at[x], send_sem=ps, recv_sem=pr,
            device_id=(zy * 4 + px, ch), device_id_type=MESH,
        )

    if POST:
        for d in range(1, 4):
            post_copy(d).start()
    post_r[x] = post_t[x]
    all_post = pltpu.make_async_remote_copy(
        src_ref=post_r.at[pl.ds(0, 3)], dst_ref=post_r.at[pl.ds(0, 3)], send_sem=ps, recv_sem=pr,
        device_id=(me, ch), device_id_type=MESH,
    )
    at("post")

    wide_low = lax.broadcasted_iota(jnp.int32, (64, 128), 1) < 64
    sign = jnp.where(wide_low, 1.0, -1.0).astype(F32)
    zero = jnp.zeros((64, 128), F32)

    def widen_a(b, carry):
        xa[pl.ds(pl.multiple_of(b * 16, 16), 16), :] = rcv_a[b].astype(F32)
        return carry

    def widen_b(b, carry):
        xb[pl.ds(pl.multiple_of(b * 8, 8), 8), :] = rcv_b[b].astype(F32)
        return carry

    def filter_half(c):
        for r in range(8):
            g = xa[pl.ds(8 + r, 64, stride=16), :]
            rg = pltpu.roll(g, 64, 1)
            own_h, oth_h = (g, rg) if c == 0 else (rg, g)
            lo = jnp.where(wide_low, own_h, zero)
            hi = jnp.where(wide_low, zero, oth_h)
            rhs = jnp.concatenate(
                [jnp.concatenate([lo, hi], 1), jnp.concatenate([-hi, -lo], 1)], 0
            ).astype(BF16)
            a = jnp.dot(cs[...], rhs, preferred_element_type=F32)
            st1[128 * r : 128 * r + 128] = (a[:, 0:128] * tw[0] + a[:, 128:256] * tw[1]).astype(BF16)
        for r in range(0, 8, 2):
            rows = slice(128 * r, 128 * r + 256)
            hf[rows, :] = jnp.dot(st1[rows, :], mid[1], preferred_element_type=F32)

    def signal_half(c):
        for r in range(8):
            v = xa[pl.ds(r, 64, stride=16), :] if c == 0 else xb[pl.ds(r, 64, stride=8), :]
            rv = pltpu.roll(v, 64, 1)
            rhs = jnp.concatenate(
                [jnp.concatenate([v, rv], 1), jnp.concatenate([rv * sign, -v * sign], 1)], 0
            ).astype(BF16)
            a = jnp.dot(cs[...], rhs, preferred_element_type=F32)
            st1[128 * r : 128 * r + 128] = (a[:, 0:128] * tw[0] + a[:, 128:256] * tw[1]).astype(BF16)
        for r in range(0, 8, 2):
            rows = slice(128 * r, 128 * r + 256)
            zz = jnp.dot(st1[rows, :], mid[0], preferred_element_type=F32)
            st2[rows, :] = (
                zz[:, 0:128] * hf[rows, 0:128] + zz[:, 128:256] * hf[rows, 128:256]
            ).astype(BF16)
        for r in range(0, 8, 2):
            m = jnp.dot(st2[128 * r : 128 * r + 256, :], mid[2], preferred_element_type=F32)
            for i in range(2):
                m0, m1 = m[128 * i : 128 * i + 128, 0:128], m[128 * i : 128 * i + 128, 128:256]
                at_row = 256 * (r + i)
                st3[at_row : at_row + 128] = (m0 * tw[0] - m1 * tw[1]).astype(BF16)
                st3[at_row + 128 : at_row + 256] = (m1 * tw[2] + m0 * tw[3]).astype(BF16)
        for r in range(8):
            of[pl.ds(r, 64, stride=8), :] = jnp.dot(
                last[...], st3[256 * r : 256 * r + 256], preferred_element_type=F32
            )

        def narrow(b, carry):
            msg2[c, b] = of[pl.ds(pl.multiple_of(b * 8, 8), 8), :].astype(BF16)
            return carry

        lax.fori_loop(0, 64, narrow, 0, unroll=8)

    def all2(c):
        return pltpu.make_async_remote_copy(
            src_ref=rcv2.at[c, pl.ds(0, 15)], dst_ref=rcv2.at[c, pl.ds(0, 15)],
            send_sem=s2.at[c], recv_sem=r2.at[c], device_id=(me, ch), device_id_type=MESH,
        )

    def give_back(c):
        def send2(k, carry):
            to = lax.rem(zy + k, 16)
            pltpu.make_async_remote_copy(
                src_ref=msg2.at[c, pl.ds(4 * to, 4)], dst_ref=rcv2.at[c, zy],
                send_sem=s2.at[c], recv_sem=r2.at[c], device_id=(to * 4 + x, ch), device_id_type=MESH,
            ).start()
            return carry

        lax.fori_loop(1, 16, send2, 0)
        rcv2[c, zy] = msg2[c, pl.ds(4 * zy, 4)]

    for i in range(5, 9):
        loads[i].wait()
    all1(0).wait_recv()
    at("recv0")
    lax.fori_loop(0, 64, widen_a, 0, unroll=8)
    filter_half(0)
    at("filter0")
    signal_half(0)
    give_back(0)
    at("back0")
    filter_half(1)
    at("filter1")
    all1(1).wait_recv()
    at("recv1")
    lax.fori_loop(0, 64, widen_b, 0, unroll=8)
    signal_half(1)
    give_back(1)
    at("back1")

    def gather(c, d):
        px = lax.rem(x + d, 4)
        mine = lhs.at[2 * x + c]
        return pltpu.make_async_remote_copy(
            src_ref=mine, dst_ref=mine, send_sem=gs.at[3 * c + d - 1], recv_sem=gr.at[3 * c + d - 1],
            device_id=(zy * 4 + px, ch), device_id_type=MESH,
        )

    gathers = [[gather(c, d) for d in range(1, 4)] for c in range(2)]
    if POST:
        all_post.wait_recv()
    for c in range(2):
        all2(c).wait_recv()
        at("ret%d" % c)
        for px in range(4):
            gt = rcv2[c, :, px].astype(F32).reshape(128, 128) * post_r[px, c].astype(F32)
            lhs[2 * x + c, 128 * px : 128 * px + 128, :] = gt.astype(BF16).astype(F32).T.astype(BF16)
        for cp in gathers[c]:
            cp.start()
        at("gather%d" % c)
    for c in range(2):
        for cp in gathers[c]:
            cp.wait_recv()
    at("matmul")

    def swap(dy):
        return pltpu.make_async_remote_copy(
            src_ref=half.at[dy], dst_ref=rcv3.at[dy], send_sem=es.at[dy], recv_sem=er.at[dy],
            device_id=(me, yl * 2 + 1 - core), device_id_type=MESH,
        )

    def project(pair, c):
        ws = []
        for dy in pair:
            y = lax.rem(yl + dy, 4)
            ws.append(wall[pl.ds(4 * y + 2 * c, 2)].reshape(128, 1024))
        rows = jnp.concatenate([lhs[i] for i in range(8)], 1)
        return lax.dot_general(
            rows, jnp.concatenate(ws, 0), (((1,), (1,)), ((), ())), preferred_element_type=F32
        )

    for pair in ((2, 1), (3, 0)):
        acc = project(pair, 1 - core)
        for i, dy in enumerate(pair):
            half[dy] = acc[:, 128 * i : 128 * i + 128].astype(BF16)
            swap(dy).start()
    for pair in ((2, 1), (3, 0)):
        acc = project(pair, core)
        for i, dy in enumerate(pair):
            own[dy] = acc[:, 128 * i : 128 * i + 128]
        for dy in pair:
            swap(dy).wait_recv()
            summ[dy] = (own[dy] + rcv3[dy].astype(F32)).astype(BF16)
            for dx in (2, 1, 3, 0):
                px = lax.rem(x + dx, 4)
                py = lax.rem(yl + dy, 4)
                piece = summ.at[dy, pl.ds(pl.multiple_of(128 * px, 128), 128)]
                if dx == 0 and dy == 0:
                    rcv4[x * 4 + yl] = piece[...]
                else:
                    pltpu.make_async_remote_copy(
                        src_ref=piece, dst_ref=rcv4.at[x * 4 + yl], send_sem=fs, recv_sem=fr,
                        device_id=(zy * 4 + px, py * 2 + core), device_id_type=MESH,
                    ).start()
    all4 = pltpu.make_async_remote_copy(
        src_ref=rcv4.at[pl.ds(0, 15)], dst_ref=rcv4.at[pl.ds(0, 15)], send_sem=fs, recv_sem=fr,
        device_id=(me, ch), device_id_type=MESH,
    )

    for c in range(2):
        all1(c).wait_send()
        all2(c).wait_send()
        for cp in gathers[c]:
            cp.wait_send()
    if WT:
        wy.wait_send()
        for cps in ring_a + ring_b:
            for cp in cps:
                cp.wait_send()
    if POST:
        all_post.wait_send()
    for y in range(4):
        swap(y).wait_send()
    all4.wait_recv()

    t = []
    for px in range(4):
        v = rcv4[4 * px].astype(F32)
        for y in range(1, 4):
            v = v + rcv4[4 * px + y].astype(F32)
        t.append(v)
    row_low = lax.broadcasted_iota(jnp.int32, (128, 128), 1) < 64
    for m in range(4):
        a, b = t[(2 * m) % 4], t[(2 * m + 1) % 4]
        if m < 2:
            o = jnp.where(row_low, a, pltpu.roll(b, 64, 1))
        else:
            o = jnp.where(row_low, pltpu.roll(a, 64, 1), b)
        o = o.astype(BF16)
        out[0, :, 128 * m : 128 * m + 128] = o[0:64]
        out[1, :, 128 * m : 128 * m + 128] = o[64:128]
    all4.wait_send()


def on_device(post_gate, pre_gate, signal, long_filter, out_weight):
    cs, tw, mid, last = tables()
    vm = pltpu.VMEM
    dma = pltpu.SemaphoreType.DMA
    scratch = [
        vm((2, 64, 1024), BF16), vm((2, 64, 1024), BF16), vm((64, 1024), BF16),
        vm((2, 64, 1024), BF16),
        vm((128, 128), BF16), vm((4, 128, 128), F32), vm((3, 128, 256), BF16), vm((64, 256), BF16),
        vm((64, 16, 128), BF16), vm((64, 16, 128), BF16),
        vm((64, 8, 128), BF16), vm((64, 8, 128), BF16),
        vm((1024, 128), F32), vm((512, 128), F32),
        vm((1024, 256), F32),
        vm((1024, 128), BF16), vm((1024, 128), BF16), vm((2048, 128), BF16),
        vm((512, 128), F32),
        vm((2, 64, 8, 128), BF16),
        vm((2, 16, 4, 8, 128), BF16),
        vm((4, 2, 128, 128), BF16), vm((4, 2, 128, 128), BF16),
        vm((8, 512, 128), BF16),
        vm((16, 64, 1024), BF16),
        vm((4, 512, 128), BF16),
        vm((4, 512, 128), BF16),
        vm((4, 512, 128), F32),
        vm((4, 512, 128), BF16),
        vm((16, 128, 128), BF16),
        dma((9,)), dma((2,)), dma((2,)), dma, dma, dma((8,)), dma((8,)), dma((8,)), dma((8,)),
        dma, dma, dma((2,)), dma((2,)), dma((6,)), dma((6,)), dma((4,)), dma((4,)), dma, dma,
    ]
    return pl.pallas_call(
        kernel,
        out_shape=jax.ShapeDtypeStruct((2, 64, 512), BF16),
        in_specs=[pl.BlockSpec(memory_space=pl.ANY)] * 9,
        out_specs=pl.BlockSpec(memory_space=pltpu.VMEM),
        scratch_shapes=scratch,
        compiler_params=pltpu.CompilerParams(
            collective_id=0, has_side_effects=True, vmem_limit_bytes=56 * 1024 * 1024
        ),
        cost_estimate=pl.CostEstimate(flops=2_000_000_000, bytes_accessed=4_000_000, transcendentals=0),
    )(pre_gate, signal, long_filter, post_gate, out_weight.T, cs, tw, mid, last)


def solution(mesh):
    return jax.shard_map(
        on_device,
        mesh=mesh,
        in_specs=(
            P(None, "ctx", "ch"),
            P(None, "ctx", "ch"),
            P(None, "ctx", "ch"),
            P("ctx", "ch"),
            P("ch", "ctx"),
        ),
        out_specs=P(None, "ctx", "ch"),
        check_vma=False,
    )
```

```python
import functools
import math

import jax
import jax.numpy as jnp
import numpy as np
from jax import lax
from jax.experimental import pallas as pl
from jax.experimental.pallas import tpu as pltpu
from jax.sharding import PartitionSpec as P

WT, POST = True, True
PLAN = {"scatter0": ("w0", "a1"), "filter0": ("a2",), "back0": ("b1",), "recv1": ("a3",), "back1": ("b2",), "gather1": ("a4", "b3"), "kn": ("b4",), "kfd": ("a5", "b5")}
MESH = pl.DeviceIdType.MESH
F32 = jnp.float32
BF16 = jnp.bfloat16


def tables():
    n1, n2, span = 128, 64, 8192
    k1 = np.arange(n1)
    b = np.arange(64)
    j = np.arange(n2)
    th = 2 * math.pi * ((k1[:, None] * b[None, :]) % n1) / n1
    cs = np.concatenate([np.cos(th), np.sin(th)], 1)
    ph = 2 * math.pi * ((k1[:, None] * j[None, :]) % span) / span
    c, s = np.cos(ph), np.sin(ph)
    tc = np.concatenate([c, c], 1)
    ts = np.concatenate([s, -s], 1)
    tcn = np.concatenate([-c, c], 1)
    tsn = np.concatenate([-s, -s], 1)
    twid = np.stack([tc, ts, tcn, tsn])
    t2 = 2 * math.pi * ((j[:, None] * j[None, :]) % n2) / n2
    c2, s2 = np.cos(t2), np.sin(t2)
    fwd = np.block([[c2, -s2, -s2, c2], [s2, c2, c2, s2]])
    filt = np.block([[c2, c2, s2, -s2], [s2, s2, -c2, c2]])
    inv = np.block([[c2, s2, s2, c2], [-s2, c2, c2, -s2]])
    mid = np.stack([fwd, filt, inv])
    last = np.concatenate([np.cos(th.T), np.sin(th.T)], 1) / span
    return (
        jnp.asarray(cs, BF16),
        jnp.asarray(twid, F32),
        jnp.asarray(mid, BF16),
        jnp.asarray(last, BF16),
    )


def kernel(
    pre_h, sig_h, fil_h, post_h, w_h, cs_h, tw_h, mid_h, last_h,
    out,
    pre, sig, fil, post, cs, tw, mid, last,
    msg_a, rcv_a, msg_b, rcv_b, xa, xb, hf, st1, st2, st3, of, msg2, rcv2, post_t, post_r,
    lhs, wall, half, rcv3, own, summ, rcv4,
    in_sem, s1, r1, wy_s, wy_r, wa_s, wa_r, wb_s, wb_r, ps, pr, s2, r2, gs, gr, es, er, fs, fr,
):
    me = lax.axis_index("ctx")
    ch = lax.axis_index("ch")
    x = lax.rem(me, 4)
    zy = me // 4
    h = lax.rem(zy, 2)
    z = zy // 2
    core = lax.rem(ch, 2)
    yl = ch // 2
    slot = x * 16 + zy

    loads = []
    for i, (src, dst) in enumerate(
        [(pre_h, pre), (sig_h, sig), (fil_h, fil), (w_h, wall.at[zy]), (post_h, post),
         (cs_h, cs), (tw_h, tw), (mid_h, mid), (last_h, last)]
    ):
        cp = pltpu.make_async_copy(src, dst, in_sem.at[i])
        cp.start()
        loads.append(cp)

    barrier = pltpu.get_barrier_semaphore()

    def greet(k, carry):
        pl.semaphore_signal(barrier, inc=1, device_id=(lax.rem(me + k, 64), ch), device_id_type=MESH)
        return carry

    lax.fori_loop(1, 64, greet, 0)

    def greet2(k, carry):
        px = lax.rem(x + lax.rem(k, 4), 4)
        py = lax.rem(yl + k // 4, 4)
        pl.semaphore_signal(
            barrier, inc=1, device_id=(zy * 4 + px, py * 2 + core), device_id_type=MESH
        )
        return carry

    lax.fori_loop(4, 16, greet2, 0)
    pl.semaphore_signal(barrier, inc=1, device_id=(me, yl * 2 + 1 - core), device_id_type=MESH)

    low = lax.broadcasted_iota(jnp.int32, (8, 128), 1) < 64

    for i in range(3):
        loads[i].wait()
    for px in range(4):
        fts = []
        for c in range(2):
            lanes = slice(256 * px + 128 * c, 256 * px + 128 * c + 128)
            v = [
                (pre[s, :, lanes].astype(F32) * sig[s, :, lanes].astype(F32)).astype(BF16).astype(F32)
                for s in range(2)
            ]
            xt = jnp.concatenate(v, 0).T
            dst = (msg_a, msg_b)[c]
            for i in range(16):
                dst[16 * px + i, 0:8, :] = xt[8 * i : 8 * i + 8].astype(BF16)
            f = fil[:, lanes].astype(F32)
            fts.append(jnp.concatenate([f, f], 0).T)
        for i in range(16):
            msg_a[16 * px + i, 8:16, :] = jnp.where(
                low, fts[0][8 * i : 8 * i + 8], fts[1][8 * i : 8 * i + 8]
            ).astype(BF16)

    pl.semaphore_wait(barrier, 76)

    msgs, rcvs = (msg_a, msg_b), (rcv_a, rcv_b)

    def all1(c):
        return pltpu.make_async_remote_copy(
            src_ref=msgs[c].at[pl.ds(0, 63)], dst_ref=rcvs[c].at[pl.ds(0, 63)],
            send_sem=s1.at[c], recv_sem=r1.at[c], device_id=(me, ch), device_id_type=MESH,
        )

    def scatter(c):
        def send1(k, carry):
            to = lax.rem(me + k, 64)
            pltpu.make_async_remote_copy(
                src_ref=msgs[c].at[lax.rem(to, 4) * 16 + to // 4], dst_ref=rcvs[c].at[me],
                send_sem=s1.at[c], recv_sem=r1.at[c], device_id=(to, ch), device_id_type=MESH,
            ).start()
            return carry

        lax.fori_loop(1, 64, send1, 0)
        rcvs[c][me] = msgs[c][slot]

    wy = pltpu.make_async_remote_copy(
        src_ref=wall.at[zy], dst_ref=wall.at[zy], send_sem=wy_s, recv_sem=wy_r,
        device_id=((zy + 1 - 2 * h) * 4 + x, ch), device_id_type=MESH,
    )

    def ring(step, hh, ssem, rsem):
        right_z, left_z = lax.rem(z + 1, 8), lax.rem(z + 7, 8)
        from_r = 2 * lax.rem(z + 9 - step, 8) + hh
        from_l = 2 * lax.rem(z + step - 1, 8) + hh
        if step < 4:
            part_r, part_l = wall.at[from_r], wall.at[from_l]
        else:
            part_r, part_l = wall.at[from_r, pl.ds(0, 32)], wall.at[from_l, pl.ds(32, 32)]
        return [
            pltpu.make_async_remote_copy(
                src_ref=part, dst_ref=part,
                send_sem=ssem.at[2 * step - 2 + i], recv_sem=rsem.at[2 * step - 2 + i],
                device_id=((to * 2 + h) * 4 + x, ch), device_id_type=MESH,
            )
            for i, (part, to) in enumerate([(part_r, right_z), (part_l, left_z)])
        ]

    ring_a = [ring(i, h, wa_s, wa_r) for i in range(1, 5)]
    ring_b = [ring(i, 1 - h, wb_s, wb_r) for i in range(1, 5)]

    def step_w(which, i):
        if not WT:
            return
        rings = ring_a if which == "a" else ring_b
        if i > 1:
            for cp in rings[i - 2]:
                cp.wait_recv()
        elif which == "b":
            wy.wait_recv()
        if i < 5:
            for cp in rings[i - 1]:
                cp.start()

    def at(name):
        for op in PLAN.get(name, ()):
            if op != "w0":
                step_w(op[0], int(op[1]))
            elif WT:
                wy.start()

    loads[3].wait()
    scatter(0)
    at("scatter0")
    scatter(1)
    at("scatter1")

    loads[4].wait()
    for px in range(4):
        for c in range(2):
            lanes = slice(256 * px + 128 * c, 256 * px + 128 * c + 128)
            pt = jnp.concatenate([post[s, :, lanes].astype(F32) for s in range(2)], 0).T
            post_t[px, c] = pt.astype(BF16)

    def post_copy(d):
        px = lax.rem(x + d, 4)
        return pltpu.make_async_remote_copy(
            src_ref=post_t.at[px], dst_ref=post_r.at[x], send_sem=ps, recv_sem=pr,
            device_id=(zy * 4 + px, ch), device_id_type=MESH,
        )

    if POST:
        for d in range(1, 4):
            post_copy(d).start()
    post_r[x] = post_t[x]
    all_post = pltpu.make_async_remote_copy(
        src_ref=post_r.at[pl.ds(0, 3)], dst_ref=post_r.at[pl.ds(0, 3)], send_sem=ps, recv_sem=pr,
        device_id=(me, ch), device_id_type=MESH,
    )
    at("post")

    wide_low = lax.broadcasted_iota(jnp.int32, (64, 128), 1) < 64
    sign = jnp.where(wide_low, 1.0, -1.0).astype(F32)
    zero = jnp.zeros((64, 128), F32)

    def widen_a(b, carry):
        xa[pl.ds(pl.multiple_of(b * 16, 16), 16), :] = rcv_a[b].astype(F32)
        return carry

    def widen_b(b, carry):
        xb[pl.ds(pl.multiple_of(b * 8, 8), 8), :] = rcv_b[b].astype(F32)
        return carry

    def filter_half(c):
        for r in range(8):
            g = xa[pl.ds(8 + r, 64, stride=16), :]
            rg = pltpu.roll(g, 64, 1)
            own_h, oth_h = (g, rg) if c == 0 else (rg, g)
            lo = jnp.where(wide_low, own_h, zero)
            hi = jnp.where(wide_low, zero, oth_h)
            rhs = jnp.concatenate(
                [jnp.concatenate([lo, hi], 1), jnp.concatenate([-hi, -lo], 1)], 0
            ).astype(BF16)
            a = jnp.dot(cs[...], rhs, preferred_element_type=F32)
            st1[128 * r : 128 * r + 128] = (a[:, 0:128] * tw[0] + a[:, 128:256] * tw[1]).astype(BF16)
        for r in range(0, 8, 2):
            rows = slice(128 * r, 128 * r + 256)
            hf[rows, :] = jnp.dot(st1[rows, :], mid[1], preferred_element_type=F32)

    def signal_half(c):
        for r in range(8):
            v = xa[pl.ds(r, 64, stride=16), :] if c == 0 else xb[pl.ds(r, 64, stride=8), :]
            rv = pltpu.roll(v, 64, 1)
            rhs = jnp.concatenate(
                [jnp.concatenate([v, rv], 1), jnp.concatenate([rv * sign, -v * sign], 1)], 0
            ).astype(BF16)
            a = jnp.dot(cs[...], rhs, preferred_element_type=F32)
            st1[128 * r : 128 * r + 128] = (a[:, 0:128] * tw[0] + a[:, 128:256] * tw[1]).astype(BF16)
        for r in range(0, 8, 2):
            rows = slice(128 * r, 128 * r + 256)
            zz = jnp.dot(st1[rows, :], mid[0], preferred_element_type=F32)
            st2[rows, :] = (
                zz[:, 0:128] * hf[rows, 0:128] + zz[:, 128:256] * hf[rows, 128:256]
            ).astype(BF16)
        for r in range(0, 8, 2):
            m = jnp.dot(st2[128 * r : 128 * r + 256, :], mid[2], preferred_element_type=F32)
            for i in range(2):
                m0, m1 = m[128 * i : 128 * i + 128, 0:128], m[128 * i : 128 * i + 128, 128:256]
                at_row = 256 * (r + i)
                st3[at_row : at_row + 128] = (m0 * tw[0] - m1 * tw[1]).astype(BF16)
                st3[at_row + 128 : at_row + 256] = (m1 * tw[2] + m0 * tw[3]).astype(BF16)
        for r in range(8):
            of[pl.ds(r, 64, stride=8), :] = jnp.dot(
                last[...], st3[256 * r : 256 * r + 256], preferred_element_type=F32
            )

        def narrow(b, carry):
            msg2[c, b] = of[pl.ds(pl.multiple_of(b * 8, 8), 8), :].astype(BF16)
            return carry

        lax.fori_loop(0, 64, narrow, 0, unroll=8)

    def all2(c):
        return pltpu.make_async_remote_copy(
            src_ref=rcv2.at[c, pl.ds(0, 15)], dst_ref=rcv2.at[c, pl.ds(0, 15)],
            send_sem=s2.at[c], recv_sem=r2.at[c], device_id=(me, ch), device_id_type=MESH,
        )

    def give_back(c):
        def send2(k, carry):
            to = lax.rem(zy + k, 16)
            pltpu.make_async_remote_copy(
                src_ref=msg2.at[c, pl.ds(4 * to, 4)], dst_ref=rcv2.at[c, zy],
                send_sem=s2.at[c], recv_sem=r2.at[c], device_id=(to * 4 + x, ch), device_id_type=MESH,
            ).start()
            return carry

        lax.fori_loop(1, 16, send2, 0)
        rcv2[c, zy] = msg2[c, pl.ds(4 * zy, 4)]

    for i in range(5, 9):
        loads[i].wait()
    all1(0).wait_recv()
    at("recv0")
    lax.fori_loop(0, 64, widen_a, 0, unroll=8)
    filter_half(0)
    at("filter0")
    signal_half(0)
    give_back(0)
    at("back0")
    filter_half(1)
    at("filter1")
    all1(1).wait_recv()
    at("recv1")
    lax.fori_loop(0, 64, widen_b, 0, unroll=8)
    signal_half(1)
    give_back(1)
    at("back1")

    def gather(c, d):
        px = lax.rem(x + d, 4)
        mine = lhs.at[2 * x + c]
        return pltpu.make_async_remote_copy(
            src_ref=mine, dst_ref=mine, send_sem=gs.at[3 * c + d - 1], recv_sem=gr.at[3 * c + d - 1],
            device_id=(zy * 4 + px, ch), device_id_type=MESH,
        )

    gathers = [[gather(c, d) for d in range(1, 4)] for c in range(2)]
    if POST:
        all_post.wait_recv()
    for c in range(2):
        all2(c).wait_recv()
        at("ret%d" % c)
        for px in range(4):
            gt = rcv2[c, :, px].astype(F32).reshape(128, 128) * post_r[px, c].astype(F32)
            lhs[2 * x + c, 128 * px : 128 * px + 128, :] = gt.astype(BF16).astype(F32).T.astype(BF16)
        for cp in gathers[c]:
            cp.start()
        at("gather%d" % c)
    for c in range(2):
        for cp in gathers[c]:
            cp.wait_recv()
    at("matmul")

    def swap(k):
        return pltpu.make_async_remote_copy(
            src_ref=half.at[k], dst_ref=rcv3.at[k], send_sem=es.at[k], recv_sem=er.at[k],
            device_id=(me, yl * 2 + 1 - core), device_id_type=MESH,
        )

    def target(k):
        return lax.rem(z // 2 + k, 4)

    def project(k):
        y = target(k)
        ws = [wall[pl.ds(4 * y + 2 * c, 2)].reshape(128, 1024) for c in (1 - core, core)]
        rows = jnp.concatenate([lhs[i] for i in range(8)], 1)
        acc = lax.dot_general(
            rows, jnp.concatenate(ws, 0), (((1,), (1,)), ((), ())), preferred_element_type=F32
        )
        half[k] = acc[:, 0:128].astype(BF16)
        swap(k).start()
        own[k] = acc[:, 128:256]

    def deliver(k):
        y = target(k)
        swap(k).wait_recv()
        summ[k] = (own[k] + rcv3[k].astype(F32)).astype(BF16)
        for dx in (2, 1, 3, 0):
            px = lax.rem(x + dx, 4)
            piece = summ.at[k, pl.ds(pl.multiple_of(128 * px, 128), 128)]

            def send(piece=piece, px=px):
                pltpu.make_async_remote_copy(
                    src_ref=piece, dst_ref=rcv4.at[x * 4 + yl], send_sem=fs, recv_sem=fr,
                    device_id=(zy * 4 + px, y * 2 + core), device_id_type=MESH,
                ).start()

            if dx:
                send()
            else:
                pl.when(y != yl)(send)

                @pl.when(y == yl)
                def _():
                    rcv4[x * 4 + yl] = piece[...]

    near = 3 - 2 * lax.rem(z, 2)
    project(0)
    at("k0")
    deliver(0)
    at("k0d")
    project(near)
    at("kn")
    deliver(near)
    at("knd")
    project(4 - near)
    at("kf")
    deliver(4 - near)
    at("kfd")
    project(2)
    deliver(2)
    all4 = pltpu.make_async_remote_copy(
        src_ref=rcv4.at[pl.ds(0, 15)], dst_ref=rcv4.at[pl.ds(0, 15)], send_sem=fs, recv_sem=fr,
        device_id=(me, ch), device_id_type=MESH,
    )

    for c in range(2):
        all1(c).wait_send()
        all2(c).wait_send()
        for cp in gathers[c]:
            cp.wait_send()
    if WT:
        wy.wait_send()
        for cps in ring_a + ring_b:
            for cp in cps:
                cp.wait_send()
    if POST:
        all_post.wait_send()
    for y in range(4):
        swap(y).wait_send()
    all4.wait_recv()

    t = []
    for px in range(4):
        v = rcv4[4 * px].astype(F32)
        for y in range(1, 4):
            v = v + rcv4[4 * px + y].astype(F32)
        t.append(v)
    row_low = lax.broadcasted_iota(jnp.int32, (128, 128), 1) < 64
    for m in range(4):
        a, b = t[(2 * m) % 4], t[(2 * m + 1) % 4]
        if m < 2:
            o = jnp.where(row_low, a, pltpu.roll(b, 64, 1))
        else:
            o = jnp.where(row_low, pltpu.roll(a, 64, 1), b)
        o = o.astype(BF16)
        out[0, :, 128 * m : 128 * m + 128] = o[0:64]
        out[1, :, 128 * m : 128 * m + 128] = o[64:128]
    all4.wait_send()


def on_device(post_gate, pre_gate, signal, long_filter, out_weight):
    cs, tw, mid, last = tables()
    vm = pltpu.VMEM
    dma = pltpu.SemaphoreType.DMA
    scratch = [
        vm((2, 64, 1024), BF16), vm((2, 64, 1024), BF16), vm((64, 1024), BF16),
        vm((2, 64, 1024), BF16),
        vm((128, 128), BF16), vm((4, 128, 128), F32), vm((3, 128, 256), BF16), vm((64, 256), BF16),
        vm((64, 16, 128), BF16), vm((64, 16, 128), BF16),
        vm((64, 8, 128), BF16), vm((64, 8, 128), BF16),
        vm((1024, 128), F32), vm((512, 128), F32),
        vm((1024, 256), F32),
        vm((1024, 128), BF16), vm((1024, 128), BF16), vm((2048, 128), BF16),
        vm((512, 128), F32),
        vm((2, 64, 8, 128), BF16),
        vm((2, 16, 4, 8, 128), BF16),
        vm((4, 2, 128, 128), BF16), vm((4, 2, 128, 128), BF16),
        vm((8, 512, 128), BF16),
        vm((16, 64, 1024), BF16),
        vm((4, 512, 128), BF16),
        vm((4, 512, 128), BF16),
        vm((4, 512, 128), F32),
        vm((4, 512, 128), BF16),
        vm((16, 128, 128), BF16),
        dma((9,)), dma((2,)), dma((2,)), dma, dma, dma((8,)), dma((8,)), dma((8,)), dma((8,)),
        dma, dma, dma((2,)), dma((2,)), dma((6,)), dma((6,)), dma((4,)), dma((4,)), dma, dma,
    ]
    return pl.pallas_call(
        kernel,
        out_shape=jax.ShapeDtypeStruct((2, 64, 512), BF16),
        in_specs=[pl.BlockSpec(memory_space=pl.ANY)] * 9,
        out_specs=pl.BlockSpec(memory_space=pltpu.VMEM),
        scratch_shapes=scratch,
        compiler_params=pltpu.CompilerParams(
            collective_id=0, has_side_effects=True, vmem_limit_bytes=56 * 1024 * 1024
        ),
        cost_estimate=pl.CostEstimate(flops=2_000_000_000, bytes_accessed=4_000_000, transcendentals=0),
    )(pre_gate, signal, long_filter, post_gate, out_weight.T, cs, tw, mid, last)


def solution(mesh):
    return jax.shard_map(
        on_device,
        mesh=mesh,
        in_specs=(
            P(None, "ctx", "ch"),
            P(None, "ctx", "ch"),
            P(None, "ctx", "ch"),
            P("ctx", "ch"),
            P("ch", "ctx"),
        ),
        out_specs=P(None, "ctx", "ch"),
        check_vma=False,
    )
```

```python
import functools
import math

import jax
import jax.numpy as jnp
import numpy as np
from jax import lax
from jax.experimental import pallas as pl
from jax.experimental.pallas import tpu as pltpu
from jax.sharding import PartitionSpec as P

WT, POST = True, True
PLAN = {"scatter0": ("w0", "a1"), "filter0": ("a2",), "back0": ("b1",), "recv1": ("a3",), "back1": ("b2",), "gather1": ("a4", "b3"), "kn": ("b4",), "kfd": ("a5", "b5")}
MESH = pl.DeviceIdType.MESH
F32 = jnp.float32
BF16 = jnp.bfloat16


def tables():
    n1, n2, span = 128, 64, 8192
    k1 = np.arange(n1)
    b = np.arange(64)
    j = np.arange(n2)
    th = 2 * math.pi * ((k1[:, None] * b[None, :]) % n1) / n1
    cs = np.concatenate([np.cos(th), np.sin(th)], 1)
    ph = 2 * math.pi * ((k1[:, None] * j[None, :]) % span) / span
    c, s = np.cos(ph), np.sin(ph)
    tc = np.concatenate([c, c], 1)
    ts = np.concatenate([s, -s], 1)
    tcn = np.concatenate([-c, c], 1)
    tsn = np.concatenate([-s, -s], 1)
    twid = np.stack([tc, ts, tcn, tsn])
    t2 = 2 * math.pi * ((j[:, None] * j[None, :]) % n2) / n2
    c2, s2 = np.cos(t2), np.sin(t2)
    fwd = np.block([[c2, -s2, -s2, c2], [s2, c2, c2, s2]])
    filt = np.block([[c2, c2, s2, -s2], [s2, s2, -c2, c2]])
    inv = np.block([[c2, s2, s2, c2], [-s2, c2, c2, -s2]])
    mid = np.stack([fwd, filt, inv])
    last = np.concatenate([np.cos(th.T), np.sin(th.T)], 1) / span
    return (
        jnp.asarray(cs, BF16),
        jnp.asarray(twid, F32),
        jnp.asarray(mid, BF16),
        jnp.asarray(last, BF16),
    )


def kernel(
    pre_h, sig_h, fil_h, post_h, w_h, cs_h, tw_h, mid_h, last_h,
    out,
    pre, sig, fil, post, cs, tw, mid, last,
    msg_a, rcv_a, msg_b, rcv_b, xa, xb, hf, st1, st2, st3, of, msg2, rcv2, post_t, post_r,
    lhs, wall, half, rcv3, own, summ, rcv4,
    in_sem, s1, r1, wy_s, wy_r, wa_s, wa_r, wb_s, wb_r, ps, pr, s2, r2, gs, gr, es, er, fs, fr,
):
    me = lax.axis_index("ctx")
    ch = lax.axis_index("ch")
    x = lax.rem(me, 4)
    zy = me // 4
    h = lax.rem(zy, 2)
    z = zy // 2
    core = lax.rem(ch, 2)
    yl = ch // 2
    slot = x * 16 + zy

    loads = []
    for i, (src, dst) in enumerate(
        [(pre_h, pre), (sig_h, sig), (fil_h, fil), (w_h, wall.at[zy]), (post_h, post),
         (cs_h, cs), (tw_h, tw), (mid_h, mid), (last_h, last)]
    ):
        cp = pltpu.make_async_copy(src, dst, in_sem.at[i])
        cp.start()
        loads.append(cp)

    barrier = pltpu.get_barrier_semaphore()

    def greet(k, carry):
        pl.semaphore_signal(barrier, inc=1, device_id=(lax.rem(me + k, 64), ch), device_id_type=MESH)
        return carry

    lax.fori_loop(1, 64, greet, 0)

    def greet2(k, carry):
        px = lax.rem(x + lax.rem(k, 4), 4)
        py = lax.rem(yl + k // 4, 4)
        pl.semaphore_signal(
            barrier, inc=1, device_id=(zy * 4 + px, py * 2 + core), device_id_type=MESH
        )
        return carry

    lax.fori_loop(4, 16, greet2, 0)
    pl.semaphore_signal(barrier, inc=1, device_id=(me, yl * 2 + 1 - core), device_id_type=MESH)

    low = lax.broadcasted_iota(jnp.int32, (8, 128), 1) < 64

    for i in range(3):
        loads[i].wait()
    for px in range(4):
        fts = []
        for c in range(2):
            lanes = slice(256 * px + 128 * c, 256 * px + 128 * c + 128)
            v = [
                (pre[s, :, lanes].astype(F32) * sig[s, :, lanes].astype(F32)).astype(BF16).astype(F32)
                for s in range(2)
            ]
            xt = jnp.concatenate(v, 0).T
            dst = (msg_a, msg_b)[c]
            for i in range(16):
                dst[16 * px + i, 0:8, :] = xt[8 * i : 8 * i + 8].astype(BF16)
            f = fil[:, lanes].astype(F32)
            fts.append(jnp.concatenate([f, f], 0).T)
        for i in range(16):
            msg_a[16 * px + i, 8:16, :] = jnp.where(
                low, fts[0][8 * i : 8 * i + 8], fts[1][8 * i : 8 * i + 8]
            ).astype(BF16)

    pl.semaphore_wait(barrier, 76)

    msgs, rcvs = (msg_a, msg_b), (rcv_a, rcv_b)

    def all1(c):
        return pltpu.make_async_remote_copy(
            src_ref=msgs[c].at[pl.ds(0, 63)], dst_ref=rcvs[c].at[pl.ds(0, 63)],
            send_sem=s1.at[c], recv_sem=r1.at[c], device_id=(me, ch), device_id_type=MESH,
        )

    def scatter(c):
        def send1(k, carry):
            to = lax.rem(me + k, 64)
            pltpu.make_async_remote_copy(
                src_ref=msgs[c].at[lax.rem(to, 4) * 16 + to // 4], dst_ref=rcvs[c].at[me],
                send_sem=s1.at[c], recv_sem=r1.at[c], device_id=(to, ch), device_id_type=MESH,
            ).start()
            return carry

        lax.fori_loop(1, 64, send1, 0)
        rcvs[c][me] = msgs[c][slot]

    wy = pltpu.make_async_remote_copy(
        src_ref=wall.at[zy], dst_ref=wall.at[zy], send_sem=wy_s, recv_sem=wy_r,
        device_id=((zy + 1 - 2 * h) * 4 + x, ch), device_id_type=MESH,
    )

    def ring(step, hh, ssem, rsem):
        right_z, left_z = lax.rem(z + 1, 8), lax.rem(z + 7, 8)
        from_r = 2 * lax.rem(z + 9 - step, 8) + hh
        from_l = 2 * lax.rem(z + step - 1, 8) + hh
        if step < 4:
            part_r, part_l = wall.at[from_r], wall.at[from_l]
        else:
            part_r, part_l = wall.at[from_r, pl.ds(0, 32)], wall.at[from_l, pl.ds(32, 32)]
        return [
            pltpu.make_async_remote_copy(
                src_ref=part, dst_ref=part,
                send_sem=ssem.at[2 * step - 2 + i], recv_sem=rsem.at[2 * step - 2 + i],
                device_id=((to * 2 + h) * 4 + x, ch), device_id_type=MESH,
            )
            for i, (part, to) in enumerate([(part_r, right_z), (part_l, left_z)])
        ]

    ring_a = [ring(i, h, wa_s, wa_r) for i in range(1, 5)]
    ring_b = [ring(i, 1 - h, wb_s, wb_r) for i in range(1, 5)]

    def step_w(which, i):
        if not WT:
            return
        rings = ring_a if which == "a" else ring_b
        if i > 1:
            for cp in rings[i - 2]:
                cp.wait_recv()
        elif which == "b":
            wy.wait_recv()
        if i < 5:
            for cp in rings[i - 1]:
                cp.start()

    def at(name):
        for op in PLAN.get(name, ()):
            if op != "w0":
                step_w(op[0], int(op[1]))
            elif WT:
                wy.start()

    loads[3].wait()
    scatter(0)
    at("scatter0")
    scatter(1)
    at("scatter1")

    loads[4].wait()
    for px in range(4):
        for c in range(2):
            lanes = slice(256 * px + 128 * c, 256 * px + 128 * c + 128)
            pt = jnp.concatenate([post[s, :, lanes].astype(F32) for s in range(2)], 0).T
            post_t[px, c] = pt.astype(BF16)

    def post_copy(d):
        px = lax.rem(x + d, 4)
        return pltpu.make_async_remote_copy(
            src_ref=post_t.at[px], dst_ref=post_r.at[x], send_sem=ps, recv_sem=pr,
            device_id=(zy * 4 + px, ch), device_id_type=MESH,
        )

    if POST:
        for d in range(1, 4):
            post_copy(d).start()
    post_r[x] = post_t[x]
    all_post = pltpu.make_async_remote_copy(
        src_ref=post_r.at[pl.ds(0, 3)], dst_ref=post_r.at[pl.ds(0, 3)], send_sem=ps, recv_sem=pr,
        device_id=(me, ch), device_id_type=MESH,
    )
    at("post")

    wide_low = lax.broadcasted_iota(jnp.int32, (64, 128), 1) < 64
    sign = jnp.where(wide_low, 1.0, -1.0).astype(F32)
    zero = jnp.zeros((64, 128), F32)

    def widen_a(b, carry):
        xa[pl.ds(pl.multiple_of(b * 16, 16), 16), :] = rcv_a[b].astype(F32)
        return carry

    def widen_b(b, carry):
        xb[pl.ds(pl.multiple_of(b * 8, 8), 8), :] = rcv_b[b].astype(F32)
        return carry

    def filter_half(c):
        for r in range(8):
            g = xa[pl.ds(8 + r, 64, stride=16), :]
            rg = pltpu.roll(g, 64, 1)
            own_h, oth_h = (g, rg) if c == 0 else (rg, g)
            lo = jnp.where(wide_low, own_h, zero)
            hi = jnp.where(wide_low, zero, oth_h)
            rhs = jnp.concatenate(
                [jnp.concatenate([lo, hi], 1), jnp.concatenate([-hi, -lo], 1)], 0
            ).astype(BF16)
            a = jnp.dot(cs[...], rhs, preferred_element_type=F32)
            st1[128 * r : 128 * r + 128] = (a[:, 0:128] * tw[0] + a[:, 128:256] * tw[1]).astype(BF16)
        for r in range(0, 8, 2):
            rows = slice(128 * r, 128 * r + 256)
            hf[rows, :] = jnp.dot(st1[rows, :], mid[1], preferred_element_type=F32)

    def signal_half(c):
        for r in range(8):
            v = xa[pl.ds(r, 64, stride=16), :] if c == 0 else xb[pl.ds(r, 64, stride=8), :]
            rv = pltpu.roll(v, 64, 1)
            rhs = jnp.concatenate(
                [jnp.concatenate([v, rv], 1), jnp.concatenate([rv * sign, -v * sign], 1)], 0
            ).astype(BF16)
            a = jnp.dot(cs[...], rhs, preferred_element_type=F32)
            st1[128 * r : 128 * r + 128] = (a[:, 0:128] * tw[0] + a[:, 128:256] * tw[1]).astype(BF16)
        for r in range(0, 8, 2):
            rows = slice(128 * r, 128 * r + 256)
            zz = jnp.dot(st1[rows, :], mid[0], preferred_element_type=F32)
            st2[rows, :] = (
                zz[:, 0:128] * hf[rows, 0:128] + zz[:, 128:256] * hf[rows, 128:256]
            ).astype(BF16)
        for r in range(0, 8, 2):
            m = jnp.dot(st2[128 * r : 128 * r + 256, :], mid[2], preferred_element_type=F32)
            for i in range(2):
                m0, m1 = m[128 * i : 128 * i + 128, 0:128], m[128 * i : 128 * i + 128, 128:256]
                at_row = 256 * (r + i)
                st3[at_row : at_row + 128] = (m0 * tw[0] - m1 * tw[1]).astype(BF16)
                st3[at_row + 128 : at_row + 256] = (m1 * tw[2] + m0 * tw[3]).astype(BF16)
        for r in range(8):
            of[pl.ds(r, 64, stride=8), :] = jnp.dot(
                last[...], st3[256 * r : 256 * r + 256], preferred_element_type=F32
            )

        def narrow(b, carry):
            msg2[c, b] = of[pl.ds(pl.multiple_of(b * 8, 8), 8), :].astype(BF16)
            return carry

        lax.fori_loop(0, 64, narrow, 0, unroll=8)

    def all2(c):
        return pltpu.make_async_remote_copy(
            src_ref=rcv2.at[c, pl.ds(0, 15)], dst_ref=rcv2.at[c, pl.ds(0, 15)],
            send_sem=s2.at[c], recv_sem=r2.at[c], device_id=(me, ch), device_id_type=MESH,
        )

    def give_back(c):
        def send2(k, carry):
            to = lax.rem(zy + k, 16)
            pltpu.make_async_remote_copy(
                src_ref=msg2.at[c, pl.ds(4 * to, 4)], dst_ref=rcv2.at[c, zy],
                send_sem=s2.at[c], recv_sem=r2.at[c], device_id=(to * 4 + x, ch), device_id_type=MESH,
            ).start()
            return carry

        lax.fori_loop(1, 16, send2, 0)
        rcv2[c, zy] = msg2[c, pl.ds(4 * zy, 4)]

    for i in range(5, 9):
        loads[i].wait()
    all1(0).wait_recv()
    at("recv0")
    lax.fori_loop(0, 64, widen_a, 0, unroll=8)
    filter_half(0)
    at("filter0")
    signal_half(0)
    give_back(0)
    at("back0")
    filter_half(1)
    at("filter1")
    all1(1).wait_recv()
    at("recv1")
    lax.fori_loop(0, 64, widen_b, 0, unroll=8)
    signal_half(1)
    give_back(1)
    at("back1")

    def gather(c, d):
        px = lax.rem(x + d, 4)
        mine = lhs.at[2 * x + c]
        return pltpu.make_async_remote_copy(
            src_ref=mine, dst_ref=mine, send_sem=gs.at[3 * c + d - 1], recv_sem=gr.at[3 * c + d - 1],
            device_id=(zy * 4 + px, ch), device_id_type=MESH,
        )

    gathers = [[gather(c, d) for d in range(1, 4)] for c in range(2)]
    if POST:
        all_post.wait_recv()
    for c in range(2):
        all2(c).wait_recv()
        at("ret%d" % c)
        for px in range(4):
            gt = rcv2[c, :, px].astype(F32).reshape(128, 128) * post_r[px, c].astype(F32)
            lhs[2 * x + c, 128 * px : 128 * px + 128, :] = gt.astype(BF16).astype(F32).T.astype(BF16)
        for cp in gathers[c]:
            cp.start()
        at("gather%d" % c)
    for c in range(2):
        for cp in gathers[c]:
            cp.wait_recv()
    at("matmul")

    def swap(k):
        return pltpu.make_async_remote_copy(
            src_ref=half.at[k], dst_ref=rcv3.at[k], send_sem=es.at[k], recv_sem=er.at[k],
            device_id=(me, yl * 2 + 1 - core), device_id_type=MESH,
        )

    def target(k):
        return lax.rem(z // 2 + k, 4)

    def project(k):
        y = target(k)
        ws = [wall[pl.ds(4 * y + 2 * c, 2)].reshape(128, 1024) for c in (1 - core, core)]
        rows = jnp.concatenate([lhs[i] for i in range(8)], 1)
        acc = lax.dot_general(
            rows, jnp.concatenate(ws, 0), (((1,), (1,)), ((), ())), preferred_element_type=F32
        )
        half[k] = acc[:, 0:128].astype(BF16)
        swap(k).start()
        own[k] = acc[:, 128:256]

    def deliver(k):
        y = target(k)
        swap(k).wait_recv()
        summ[k] = (own[k] + rcv3[k].astype(F32)).astype(BF16)
        for dx in (2, 1, 3, 0):
            px = lax.rem(x + dx, 4)
            piece = summ.at[k, pl.ds(pl.multiple_of(128 * px, 128), 128)]

            def send(piece=piece, px=px):
                pltpu.make_async_remote_copy(
                    src_ref=piece, dst_ref=rcv4.at[x * 4 + yl], send_sem=fs, recv_sem=fr,
                    device_id=(zy * 4 + px, y * 2 + core), device_id_type=MESH,
                ).start()

            if dx:
                send()
            else:
                pl.when(y != yl)(send)

                @pl.when(y == yl)
                def _():
                    rcv4[x * 4 + yl] = piece[...]

    near = 3 - 2 * lax.rem(z, 2)
    project(0)
    project(near)
    deliver(0)
    at("kn")
    deliver(near)
    at("knd")
    project(4 - near)
    at("kf")
    deliver(4 - near)
    at("kfd")
    project(2)
    deliver(2)
    all4 = pltpu.make_async_remote_copy(
        src_ref=rcv4.at[pl.ds(0, 15)], dst_ref=rcv4.at[pl.ds(0, 15)], send_sem=fs, recv_sem=fr,
        device_id=(me, ch), device_id_type=MESH,
    )

    for c in range(2):
        all1(c).wait_send()
        all2(c).wait_send()
        for cp in gathers[c]:
            cp.wait_send()
    if WT:
        wy.wait_send()
        for cps in ring_a + ring_b:
            for cp in cps:
                cp.wait_send()
    if POST:
        all_post.wait_send()
    for y in range(4):
        swap(y).wait_send()
    all4.wait_recv()

    t = []
    for px in range(4):
        v = rcv4[4 * px].astype(F32)
        for y in range(1, 4):
            v = v + rcv4[4 * px + y].astype(F32)
        t.append(v)
    row_low = lax.broadcasted_iota(jnp.int32, (128, 128), 1) < 64
    for m in range(4):
        a, b = t[(2 * m) % 4], t[(2 * m + 1) % 4]
        if m < 2:
            o = jnp.where(row_low, a, pltpu.roll(b, 64, 1))
        else:
            o = jnp.where(row_low, pltpu.roll(a, 64, 1), b)
        o = o.astype(BF16)
        out[0, :, 128 * m : 128 * m + 128] = o[0:64]
        out[1, :, 128 * m : 128 * m + 128] = o[64:128]
    all4.wait_send()


def on_device(post_gate, pre_gate, signal, long_filter, out_weight):
    cs, tw, mid, last = tables()
    vm = pltpu.VMEM
    dma = pltpu.SemaphoreType.DMA
    scratch = [
        vm((2, 64, 1024), BF16), vm((2, 64, 1024), BF16), vm((64, 1024), BF16),
        vm((2, 64, 1024), BF16),
        vm((128, 128), BF16), vm((4, 128, 128), F32), vm((3, 128, 256), BF16), vm((64, 256), BF16),
        vm((64, 16, 128), BF16), vm((64, 16, 128), BF16),
        vm((64, 8, 128), BF16), vm((64, 8, 128), BF16),
        vm((1040, 128), F32), vm((520, 128), F32),
        vm((1024, 256), F32),
        vm((1024, 128), BF16), vm((1024, 128), BF16), vm((2048, 128), BF16),
        vm((520, 128), F32),
        vm((2, 64, 8, 128), BF16),
        vm((2, 16, 4, 8, 128), BF16),
        vm((4, 2, 128, 128), BF16), vm((4, 2, 128, 128), BF16),
        vm((8, 512, 128), BF16),
        vm((16, 64, 1024), BF16),
        vm((4, 512, 128), BF16),
        vm((4, 512, 128), BF16),
        vm((4, 512, 128), F32),
        vm((4, 512, 128), BF16),
        vm((16, 128, 128), BF16),
        dma((9,)), dma((2,)), dma((2,)), dma, dma, dma((8,)), dma((8,)), dma((8,)), dma((8,)),
        dma, dma, dma((2,)), dma((2,)), dma((6,)), dma((6,)), dma((4,)), dma((4,)), dma, dma,
    ]
    return pl.pallas_call(
        kernel,
        out_shape=jax.ShapeDtypeStruct((2, 64, 512), BF16),
        in_specs=[pl.BlockSpec(memory_space=pl.ANY)] * 9,
        out_specs=pl.BlockSpec(memory_space=pltpu.VMEM),
        scratch_shapes=scratch,
        compiler_params=pltpu.CompilerParams(
            collective_id=0, has_side_effects=True, vmem_limit_bytes=56 * 1024 * 1024
        ),
        cost_estimate=pl.CostEstimate(flops=2_000_000_000, bytes_accessed=4_000_000, transcendentals=0),
    )(pre_gate, signal, long_filter, post_gate, out_weight.T, cs, tw, mid, last)


def solution(mesh):
    return jax.shard_map(
        on_device,
        mesh=mesh,
        in_specs=(
            P(None, "ctx", "ch"),
            P(None, "ctx", "ch"),
            P(None, "ctx", "ch"),
            P("ctx", "ch"),
            P("ch", "ctx"),
        ),
        out_specs=P(None, "ctx", "ch"),
        check_vma=False,
    )
```
